256 devices in a mesh: blk: 16 (over z, y_hi), labels: 16 (over x, y_lo, core).
Axes of the slice: x: 4, y: 4 (y_hi: 2, y_lo: 2; y = y_hi * 2 + y_lo), z: 8, core: 2. Of those that a mesh axis runs over, the one named last changes fastest.
Arguments:
- features: bfloat16 [12288, 4096], P('blk'), may hold values from -0.099609375 to 0.099609375
- positives: int32 [12288, 8], P('blk'), may hold values from 0 to 131071
- tile_rows: int32 [1024, 4], P(('labels', 'blk')), may hold values from 0 to 31, as said below
- tile_count: int32 [1024], P(('labels', 'blk')), may hold values from 1 to 4, as said below
- weight: float32 [1024, 4, 128, 128], P(('labels', 'blk')), may hold values from -96 to 96
- first_moment: float32 [1024, 4, 128, 128], P(('labels', 'blk')), may hold values from -3 to 3
- second_moment: float32 [1024, 4, 128, 128], P(('labels', 'blk')), may hold values from 0.05 to 2
Outputs:
- new_weight: float32 [1024, 4, 128, 128], P(('labels', 'blk'))
- new_first: float32 [1024, 4, 128, 128], P(('labels', 'blk'))
- new_second: float32 [1024, 4, 128, 128], P(('labels', 'blk'))
The draws below stay inside these ranges and needn't reach their ends.
Inputs may be any that keep to these rules, and one draw needn't show every extreme that they name: `tile_rows`: in each column block the 4 entries are distinct tile rows; only the first tile_count entries name kept tiles. `tile_count`: every column block keeps at least one tile.
All inputs are finite; a program needn't handle non-finite values.
Results may differ from the reference program's by a relative error of at most 0.0003.
Values may be sent and summed in bfloat16 or wider, within the bound.
No kernel may reach another device: no remote copies, remote signals or barrier semaphores. Data moves between devices by JAX's collectives and lax.ppermute only.
A program may use at most 64 MiB of HBM per device.

```python
import math
import jax
import jax.numpy as jnp
import numpy as np
from jax import lax

D = 4096
TILE = 128
KMAX = 4
POS = 8
TILE_ROWS = 32
NCB = 1024
LABELS = 131072
ROWS = 12288


def draw_tile_rows(key, part):
    scores = jax.random.randint(key, (NCB, TILE_ROWS), 0, 2 ** 20) * TILE_ROWS
    scores = scores + jnp.arange(TILE_ROWS, dtype=jnp.int32)[None, :]
    order = jnp.argsort(scores, axis=1)
    return order[:, :KMAX].astype(jnp.int32)


def draw_tile_count(key, part):
    counts = jax.random.randint(key, (NCB,), 1, KMAX + 1)
    spot = jax.random.randint(jax.random.fold_in(key, 7), (), 0, NCB)
    return counts.at[spot].set(KMAX).astype(jnp.int32)


def with_ends(result, own_key, smallest, high):
    index_at = [jax.random.randint(jax.random.fold_in(own_key, axis), (), 0, length) for axis, length in enumerate(result.shape)]
    widest = result.shape.index(max(result.shape))
    beside = index_at[:widest] + [(index_at[widest] + 1) % result.shape[widest]] + index_at[widest + 1:]
    return result.at[tuple(index_at)].set(smallest).at[tuple(beside)].set(high)


def steps_of(rng, shape, split, smallest, high):
    loudness = 1.0
    for dim, shards_of in split:
        draws = jax.random.uniform(jax.random.fold_in(jax.random.fold_in(rng, 6), dim), (shards_of,), jnp.float32, smallest / len(split), high / len(split))
        loudness = loudness * jnp.repeat(jnp.exp(draws), shape[dim] // shards_of).reshape((-1,) + (1,) * (len(shape) - 1 - dim))
    return loudness


def ranked_wide(key, dims, amount, skew):
    weights = [min(1 << octave, amount + 1 - (1 << octave)) * (1 << 20) // math.isqrt((1 << octave) ** skew) + 1 for octave in range((amount + 1).bit_length()) if 1 << octave <= amount]
    width = 1 + sum(weights) // (1 << 30)
    grid = np.cumsum(np.array([max(1, weight // width) for weight in weights]))
    lot = jax.random.randint(jax.random.fold_in(key, 1), dims, 0, int(grid[len(weights) - 1]))
    start = jnp.left_shift(1, jnp.searchsorted(jnp.asarray(grid, jnp.int32), lot, side="right").astype(jnp.int32))
    grade = start - 1 + jax.random.randint(jax.random.fold_in(key, 4), dims, 0, 1 << 30) % jnp.minimum(start, amount + 1 - start)
    return jax.random.permutation(jax.random.fold_in(key, 2), amount)[grade].astype(jnp.int32)


def scatter_about(own_key, extent, deviation, reach, cuts=(), kind=jnp.bfloat16):
    result = deviation * jax.random.normal(own_key, extent, jnp.float32)
    if cuts:
        result = result * steps_of(own_key, extent, cuts, -0.22, 0.18)
    return jnp.clip(result, -reach, reach).astype(kind)


def setup_inputs(seed: int = 0) -> dict:
    arg_keys = jax.random.split(jax.random.key(seed), 8)
    return {
        "features": scatter_about(arg_keys[0], (ROWS, D), 0.015625, 0.099609375, ((0, 16),)),
        "positives": with_ends(ranked_wide(arg_keys[1], (ROWS, POS), LABELS, 2), jax.random.fold_in(arg_keys[1], 3), 0, LABELS - 1).astype(jnp.int32),
        "tile_rows": draw_tile_rows(jax.random.fold_in(arg_keys[7], 71), 0),
        "tile_count": draw_tile_count(jax.random.fold_in(arg_keys[7], 71), 0),
        "weight": scatter_about(arg_keys[4], (NCB, KMAX, TILE, TILE), 16.0, 96.0, ((0, 256),), jnp.float32),
        "first_moment": scatter_about(arg_keys[5], (NCB, KMAX, TILE, TILE), 0.5, 3.0, ((0, 256),), jnp.float32),
        "second_moment": jnp.clip(jnp.exp(math.log(2.0) - 3.6888794 * jax.random.uniform(arg_keys[6], (NCB, KMAX, TILE, TILE), jnp.float32) ** steps_of(arg_keys[6], (NCB, KMAX, TILE, TILE), ((0, 256),), -0.2, 0.2)), 0.05, 2.0),
    }


beta_one = 0.9
beta_two = 0.999
adam_eps = 1e-08
learn_rate = 0.1
correction_one = 1.0 - 0.9 ** 10
correction_two = 1.0 - 0.999 ** 10

def reference(features, positives, tile_rows, tile_count, weight, first_moment, second_moment):
    total_rows = features.shape[0]
    tile_split = features.reshape(total_rows, D // TILE, TILE)
    slot_ids = jnp.arange(KMAX, dtype=jnp.int32)

    def one_block(block_args):
        block_index, row_ids, slot_count, block_weight = block_args
        live_mask = (slot_ids < slot_count).astype(jnp.float32)
        chosen = jnp.take(tile_split, row_ids.astype(jnp.int32), axis=1).astype(jnp.float32)
        rounded = lax.optimization_barrier(block_weight.astype(jnp.bfloat16))
        w_masked = rounded.astype(jnp.float32) * live_mask[:, None, None]
        logits = jnp.einsum('rsk,skt->rt', chosen, w_masked)
        label_ids = block_index * TILE + jnp.arange(TILE, dtype=jnp.int32)
        targets = jnp.any(positives[:, :, None] == label_ids[None, None, :], axis=1).astype(jnp.float32)
        residual = lax.optimization_barrier((jax.nn.sigmoid(logits) - targets).astype(jnp.bfloat16))
        return jnp.einsum('rsk,rt->skt', chosen, residual.astype(jnp.float32))
    gradient = lax.map(one_block, (jnp.arange(NCB, dtype=jnp.int32), tile_rows, tile_count, weight))
    kept = (slot_ids[None, :] < tile_count[:, None])[:, :, None, None]
    moved_first = beta_one * first_moment + (1.0 - beta_one) * gradient
    moved_second = beta_two * second_moment + (1.0 - beta_two) * gradient * gradient
    step_dir = moved_first / correction_one / (jnp.sqrt(moved_second / correction_two) + adam_eps)
    moved_weight = weight - learn_rate * step_dir
    new_weight = jnp.where(kept, moved_weight, weight)
    new_first = jnp.where(kept, moved_first, first_moment)
    new_second = jnp.where(kept, moved_second, second_moment)
    return (new_weight, new_first, new_second)
```

```python
import functools
import math

import jax
import jax.numpy as jnp
from jax import lax
from jax.experimental import pallas as pl
from jax.experimental.pallas import tpu as pltpu
from jax.sharding import PartitionSpec as P

beta_one = 0.9
beta_two = 0.999
adam_eps = 1e-08
learn_rate = 0.1
correction_one = 1.0 - 0.9**10
correction_two = 1.0 - 0.999**10

STEPS = 8.0
TOP = 32000.0
LN2 = math.log(2.0)
CODE_ROWS = 16
FIELDS = 8


def z_shift(array, by, z_size):
    moves = [(2 * z + h, 2 * ((z + by) % z_size) + h) for z in range(z_size) for h in range(2)]
    return lax.ppermute(array, "blk", moves)


def cross_moves(z_size, label_size):
    return [
        ((2 * z + h) * label_size + l, (2 * z + 1 - h) * label_size + (l ^ 2))
        for z in range(z_size)
        for h in range(2)
        for l in range(label_size)
    ]


def grad_kernel(with_acc, first, table, x0, x1, x2, x3, pos, w, *rest):
    acc, out = rest if with_acc else (None, rest[0])
    here = first + pl.program_id(0)
    base = table[here * FIELDS + 4]
    x = jnp.concatenate([x0[...], x1[...], x2[...], x3[...]], axis=1)
    w_t = w[0].T
    logits = lax.dot_general(w_t, x, (((1,), (1,)), ((), ())), preferred_element_type=jnp.float32)
    rel = pos[...] - base
    word_of = rel >> 5
    bit = jnp.left_shift(jnp.int32(1), rel & 31)
    sub = lax.broadcasted_iota(jnp.int32, rel.shape, 0)
    hits = []
    for word in range(4):
        m = jnp.where(word_of == word, bit, 0)
        for by in (4, 2, 1):
            m = m | pltpu.roll(m, by, 0)
        for part in range(4):
            hits.append(lax.shift_right_logical(m, sub + 8 * part) & 1)
    targets = jnp.concatenate(hits, axis=0).astype(jnp.float32)
    resid = (1.0 / (1.0 + jnp.exp(-logits)) - targets).astype(jnp.bfloat16)
    grad = jnp.dot(resid, x, preferred_element_type=jnp.float32)
    out[0] = grad if acc is None else acc[0] + grad


def tile_grad(table, x, pos, w, first, acc=None, acc_first=0):
    rows = x.shape[0]
    blocks, depth, side = w.shape
    slot_specs = [
        pl.BlockSpec((rows, side), functools.partial(lambda s, b, t: (0, t[(first + b) * FIELDS + s]), s))
        for s in range(4)
    ]
    specs = slot_specs + [
        pl.BlockSpec(pos.shape, lambda b, t: (0, 0)),
        pl.BlockSpec((1, depth, side), lambda b, t: (b, 0, 0)),
    ]
    operands = [x, x, x, x, pos, w]
    if acc is not None:
        specs.append(pl.BlockSpec((1, side, depth), lambda b, t: (b + acc_first, 0, 0)))
        operands.append(acc)
    return pl.pallas_call(
        functools.partial(grad_kernel, acc is not None, first),
        out_shape=jax.ShapeDtypeStruct((blocks, side, depth), jnp.float32),
        grid_spec=pltpu.PrefetchScalarGridSpec(
            num_scalar_prefetch=1,
            grid=(blocks,),
            in_specs=specs,
            out_specs=pl.BlockSpec((1, side, depth), lambda b, t: (b, 0, 0)),
        ),
        compiler_params=pltpu.CompilerParams(vmem_limit_bytes=32 * 1024 * 1024),
        cost_estimate=pl.CostEstimate(
            flops=8 * blocks * rows * depth * side,
            bytes_accessed=2 * blocks * rows * depth,
            transcendentals=2 * blocks * rows * side,
        ),
        name="tile_grad",
    )(table, *operands)


def decoded(q, codes):
    scale = jnp.exp(codes.astype(jnp.float32) * (LN2 / STEPS)) * (1.0 / TOP)
    return q.astype(jnp.int32).astype(jnp.float32) * scale


def encode_kernel(with_got, *refs):
    grad, out = refs[-2], refs[-1]
    side = grad.shape[1]
    total = 2 * side
    row = lax.broadcasted_iota(jnp.int32, (CODE_ROWS, grad.shape[2]), 0)
    codes = jnp.zeros((CODE_ROWS, grad.shape[2]), jnp.int32)
    if with_got:
        got = refs[0]
        got_codes = got[total : total + CODE_ROWS, :].astype(jnp.int32)
    for b in range(2):
        g = grad[b]
        if with_got:
            g = g + decoded(got[side * b : side * (b + 1), :], got_codes[b : b + 1])
        top = jnp.maximum(jnp.max(jnp.abs(g), axis=0, keepdims=True), 1e-30)
        code = jnp.ceil(jnp.log(top) * (STEPS / LN2))
        q = jnp.round(g * (jnp.exp(code * (-LN2 / STEPS)) * TOP))
        out[side * b : side * (b + 1), :] = q.astype(jnp.int32).astype(jnp.int16)
        codes = jnp.where(row == b, code.astype(jnp.int32), codes)
    out[total : total + CODE_ROWS, :] = codes.astype(jnp.int16)


def encode(grad, half, got=None):
    side, depth = grad.shape[1:]
    rows = 2 * side + CODE_ROWS
    whole = pl.BlockSpec((rows, depth), lambda i: (0, 0))
    specs = [pl.BlockSpec((2, side, depth), lambda i: (half, 0, 0))]
    operands = [grad]
    if got is not None:
        specs.insert(0, whole)
        operands.insert(0, got)
    return pl.pallas_call(
        functools.partial(encode_kernel, got is not None),
        out_shape=jax.ShapeDtypeStruct((rows, depth), jnp.int16),
        grid=(1,),
        in_specs=specs,
        out_specs=whole,
        compiler_params=pltpu.CompilerParams(vmem_limit_bytes=32 * 1024 * 1024),
        cost_estimate=pl.CostEstimate(flops=20 * rows * depth, bytes_accessed=8 * rows * depth, transcendentals=0),
        name="encode",
    )(*operands)


def adam_kernel(table, grad, low_a, low_b, high_a, high_b, weight, first, second, new_weight, new_first, new_second):
    b = pl.program_id(0)
    side = grad.shape[1]
    second_half, odd = b >= 2, b % 2
    start = pl.multiple_of(odd * side, side)
    total = grad[0]
    for first_msg, second_msg in ((low_a, low_b), (high_a, high_b)):
        q = jnp.where(
            second_half,
            second_msg[pl.ds(start, side), :].astype(jnp.int32),
            first_msg[pl.ds(start, side), :].astype(jnp.int32),
        )
        codes = jnp.where(
            second_half,
            second_msg[2 * side : 2 * side + CODE_ROWS, :].astype(jnp.int32),
            first_msg[2 * side : 2 * side + CODE_ROWS, :].astype(jnp.int32),
        )
        total = total + decoded(q, jnp.where(odd == 1, codes[1:2], codes[0:1]))
    count = table[b * FIELDS + 5]
    for s in range(4):
        g = total[:, s * side : (s + 1) * side].T
        kept = s < count
        m, v, w = first[0, s], second[0, s], weight[0, s]
        moved_first = beta_one * m + (1.0 - beta_one) * g
        moved_second = beta_two * v + (1.0 - beta_two) * g * g
        step_dir = moved_first / correction_one / (jnp.sqrt(moved_second / correction_two) + adam_eps)
        new_first[0, s] = jnp.where(kept, moved_first, m)
        new_second[0, s] = jnp.where(kept, moved_second, v)
        new_weight[0, s] = jnp.where(kept, w - learn_rate * step_dir, w)


def adam(table, grad, low_a, low_b, high_a, high_b, weight, first, second):
    blocks, slots, side = weight.shape[:3]
    msg = pl.BlockSpec(low_a.shape, lambda b, t: (0, 0))
    state = pl.BlockSpec((1,) + weight.shape[1:], lambda b, t: (b, 0, 0, 0))
    out = jax.ShapeDtypeStruct(weight.shape, jnp.float32)
    return pl.pallas_call(
        adam_kernel,
        out_shape=(out, out, out),
        grid_spec=pltpu.PrefetchScalarGridSpec(
            num_scalar_prefetch=1,
            grid=(blocks,),
            in_specs=[pl.BlockSpec((1, side, slots * side), lambda b, t: (b, 0, 0))] + [msg] * 4 + [state] * 3,
            out_specs=(state, state, state),
        ),
        compiler_params=pltpu.CompilerParams(vmem_limit_bytes=32 * 1024 * 1024),
        name="adam",
    )(table, grad, low_a, low_b, high_a, high_b, weight, first, second)


def local(features, positives, tile_rows, tile_count, weight, first_moment, second_moment):
    blocks, slots, side = weight.shape[:3]
    rows = features.shape[0]
    z_size = lax.axis_size("blk") // 2
    label_size = lax.axis_size("labels")
    shift = functools.partial(z_shift, z_size=z_size)
    blk, label = lax.axis_index("blk"), lax.axis_index("labels")
    crossing = cross_moves(z_size, label_size)

    with jax.named_scope("tables"):
        base = ((label * lax.axis_size("blk") + blk) * blocks + jnp.arange(blocks, dtype=jnp.int32)) * side
        fields = [tile_rows, base[:, None], tile_count[:, None], jnp.zeros((blocks, 2), jnp.int32)]
        own_table = jnp.concatenate(fields, axis=1)[None]
        table = own_table
        for by in (1, 2, 4):
            table = jnp.concatenate([table, shift(table, by)], axis=0)
        table = table.reshape(-1)
        own_table = own_table.reshape(-1)

    with jax.named_scope("rows_of_other_half"):
        part = rows // label_size
        piece = lax.dynamic_slice_in_dim(features, (label ^ 2) * part, part, 0)
        piece = lax.ppermute(piece, ("blk", "labels"), crossing)
        other = lax.all_gather(piece, "labels", axis=0, tiled=True)
        own_pos = positives.T
        other_pos = lax.ppermute(own_pos, ("blk", "labels"), crossing)

    with jax.named_scope("kept_tiles"):
        kept = jnp.arange(slots, dtype=jnp.int32)[None, :] < tile_count[:, None]
        tiles = jnp.where(kept[:, :, None, None], weight, 0.0).astype(jnp.bfloat16)
        tiles = tiles.reshape(blocks, slots * side, side)

    with jax.named_scope("tiles_round_z"):
        ring = {0: tiles}
        up, down = tiles, tiles
        for hop in (1, 2, 3):
            up, down = shift(up, 1), shift(down, -1)
            ring[hop], ring[z_size - hop] = up, down
        far = (shift(up[:2], 1), shift(down[2:], -1))

    with jax.named_scope("own_rows"):
        part_sum = {}
        for j in (0, 1, 7, 2, 6, 3, 5):
            part_sum[j] = tile_grad(table, features, own_pos, ring[j], j * blocks)
        far_sum = [tile_grad(table, features, own_pos, far[i], 4 * blocks + 2 * i) for i in range(2)]

    with jax.named_scope("other_rows"):
        full = {}
        far_full = [
            tile_grad(table, other, other_pos, far[i], 4 * blocks + 2 * i, far_sum[i]) for i in range(2)
        ]
        for j in (5, 3, 6, 2, 7, 1, 0):
            full[j] = tile_grad(table, other, other_pos, ring[j], j * blocks, part_sum[j])

    with jax.named_scope("sums_round_z"):
        down_a, up_b = encode(far_full[0], 0), encode(far_full[1], 0)
        down_b = up_a = None
        for hop in (3, 2, 1):
            down_a, up_b = shift(down_a, -1), shift(up_b, 1)
            if down_b is not None:
                down_b, up_a = shift(down_b, -1), shift(up_a, 1)
            down_b, up_a = encode(full[hop], 1, down_b), encode(full[z_size - hop], 0, up_a)
            down_a, up_b = encode(full[hop], 0, down_a), encode(full[z_size - hop], 1, up_b)
        down_a, up_b = shift(down_a, -1), shift(up_b, 1)
        down_b, up_a = shift(down_b, -1), shift(up_a, 1)

    with jax.named_scope("adam"):
        return tuple(
            adam(own_table, full[0], down_a, down_b, up_a, up_b, weight, first_moment, second_moment)
        )


def solution(mesh):
    whole = P(("labels", "blk"), None, None, None)
    return jax.shard_map(
        local,
        mesh=mesh,
        in_specs=(
            P("blk", None),
            P("blk", None),
            P(("labels", "blk"), None),
            P(("labels", "blk")),
            whole,
            whole,
            whole,
        ),
        out_specs=(whole, whole, whole),
        check_vma=False,
    )
```

```python
import functools
import math

import jax
import jax.numpy as jnp
from jax import lax
from jax.experimental import pallas as pl
from jax.experimental.pallas import tpu as pltpu
from jax.sharding import PartitionSpec as P

beta_one = 0.9
beta_two = 0.999
adam_eps = 1e-08
learn_rate = 0.1
correction_one = 1.0 - 0.9**10
correction_two = 1.0 - 0.999**10

STEPS = 8.0
TOP = 32000.0
LN2 = math.log(2.0)
CODE_ROWS = 16
VMEM_LIMIT = 16 * 1024 * 1024


def z_shift(array, by, z_size):
    moves = [(2 * z + h, 2 * ((z + by) % z_size) + h) for z in range(z_size) for h in range(2)]
    return lax.ppermute(array, "blk", moves)


def moved(array, z_size, label_size, cross=False, x_by=0, swap=False):
    moves = []
    for blk in range(2 * z_size):
        for l in range(label_size):
            x, y_lo, core = l // 4, l // 2 % 2, l % 2
            to = ((x + x_by) % (label_size // 4)) * 4 + (y_lo ^ cross) * 2 + (core ^ swap)
            moves.append((blk * label_size + l, (blk ^ cross) * label_size + to))
    return lax.ppermute(array, ("blk", "labels"), moves)


def in_vmem(array):
    return pltpu.with_memory_space_constraint(array, pltpu.VMEM)


def code_of(g):
    top = jnp.maximum(jnp.max(jnp.abs(g), axis=0, keepdims=True), 1e-30)
    return jnp.ceil(jnp.log(top) * (STEPS / LN2))


def coded(g, code):
    q = jnp.round(g * (jnp.exp(code * (-LN2 / STEPS)) * TOP))
    return q.astype(jnp.int32).astype(jnp.int16)


def decoded(q, codes):
    scale = jnp.exp(codes.astype(jnp.float32) * (LN2 / STEPS)) * (1.0 / TOP)
    return q.astype(jnp.int32).astype(jnp.float32) * scale


def store_half(out, grads):
    if out.dtype == jnp.float32:
        for b, g in enumerate(grads):
            out[b] = g
        return
    side, depth = grads[0].shape
    row = lax.broadcasted_iota(jnp.int32, (CODE_ROWS, depth), 0)
    codes = jnp.zeros((CODE_ROWS, depth), jnp.int32)
    for b, g in enumerate(grads):
        code = code_of(g)
        out[side * b : side * (b + 1), :] = coded(g, code)
        codes = jnp.where(row == b, code.astype(jnp.int32), codes)
    out[2 * side : 2 * side + CODE_ROWS, :] = codes.astype(jnp.int16)


def residual(w_t, x, pos, base):
    logits = lax.dot_general(w_t, x, (((1,), (1,)), ((), ())), preferred_element_type=jnp.float32)
    rel = pos - base
    word_of = rel >> 5
    bit = jnp.left_shift(jnp.int32(1), rel & 31)
    sub = lax.broadcasted_iota(jnp.int32, rel.shape, 0)
    hits = []
    for word in range(4):
        m = jnp.where(word_of == word, bit, 0)
        for by in (4, 2, 1):
            m = m | pltpu.roll(m, by, 0)
        for part in range(4):
            hits.append(lax.shift_right_logical(m, sub + 8 * part) & 1)
    targets = jnp.concatenate(hits, axis=0).astype(jnp.float32)
    return (1.0 / (1.0 + jnp.exp(-logits)) - targets).astype(jnp.bfloat16)


def grad_kernel(slabs, n_tiles, with_acc, *refs):
    table, refs = refs[0], refs[1:]
    rows = []
    for pieces in slabs:
        rows.append((refs[:pieces], refs[pieces]))
        refs = refs[pieces + 1 :]
    tiles, refs = refs[:n_tiles], refs[n_tiles:]
    accs, outs = (refs[:2], refs[2:]) if with_acc else ((None, None), refs)
    side = tiles[0].shape[1]
    depth = 4 * side
    for half in range(2):
        grads = []
        for b in range(2):
            block = 2 * half + b
            columns = [pl.ds(pl.multiple_of(table[block * 4 + s] * side, side), side) for s in range(4)]
            if n_tiles == 2:
                w = tiles[half][b * depth : (b + 1) * depth, :]
            else:
                start = block * depth + (CODE_ROWS if half else 0)
                w = tiles[0][start : start + depth, :]
            w_t = w.T
            grad = accs[half][b] if with_acc else None
            for pieces, pos in rows:
                x = jnp.concatenate(
                    [jnp.concatenate([piece[:, c] for c in columns], axis=1) for piece in pieces], axis=0
                )
                term = jnp.dot(
                    residual(w_t, x, pos[...], table[16] + block * side), x, preferred_element_type=jnp.float32
                )
                grad = term if grad is None else grad + term
            grads.append(grad)
        store_half(outs[half], grads)


def tile_grads(table, slabs, tiles, acc=None, as_message=(False, False)):
    vmem = pl.BlockSpec(memory_space=pltpu.VMEM)
    operands = []
    for pieces, pos in slabs:
        operands += [in_vmem(piece) for piece in pieces] + [pos]
    operands += tiles
    if acc is not None:
        operands += acc
    side = tiles[0].shape[1]
    depth = 4 * side
    rows = sum(pos.shape[1] for _, pos in slabs)
    return pl.pallas_call(
        functools.partial(grad_kernel, [len(p) for p, _ in slabs], len(tiles), acc is not None),
        out_shape=[
            jax.ShapeDtypeStruct((2 * side + CODE_ROWS, depth), jnp.int16)
            if message
            else jax.ShapeDtypeStruct((2, side, depth), jnp.float32)
            for message in as_message
        ],
        in_specs=[pl.BlockSpec(memory_space=pltpu.SMEM)] + [vmem] * len(operands),
        out_specs=[vmem, vmem],
        compiler_params=pltpu.CompilerParams(vmem_limit_bytes=VMEM_LIMIT),
        cost_estimate=pl.CostEstimate(flops=48 * rows * depth * side, bytes_accessed=1 << 20, transcendentals=0),
        name="tile_grads",
    )(table, *operands)


def encode_kernel(got, grad, out):
    side = grad.shape[1]
    got_codes = got[2 * side : 2 * side + CODE_ROWS, :].astype(jnp.int32)
    store_half(
        out, [grad[b] + decoded(got[side * b : side * (b + 1), :], got_codes[b : b + 1]) for b in range(2)]
    )


def encode(got, grad):
    vmem = pl.BlockSpec(memory_space=pltpu.VMEM)
    return pl.pallas_call(
        encode_kernel,
        out_shape=jax.ShapeDtypeStruct(got.shape, jnp.int16),
        in_specs=[vmem, vmem],
        out_specs=vmem,
        compiler_params=pltpu.CompilerParams(vmem_limit_bytes=VMEM_LIMIT),
        cost_estimate=pl.CostEstimate(flops=0, bytes_accessed=3 << 20, transcendentals=0),
        name="encode",
    )(got, grad)


def adam_kernel(counts, grad_a, grad_b, low_a, low_b, high_a, high_b, weight, first, second, new_weight, new_first, new_second):
    b = pl.program_id(0)
    side = grad_a.shape[1]
    second_half, odd = b >= 2, b % 2
    start = pl.multiple_of(odd * side, side)
    total = jnp.where(second_half, grad_b[odd], grad_a[odd])
    for first_msg, second_msg in ((low_a, low_b), (high_a, high_b)):
        q = jnp.where(
            second_half,
            second_msg[pl.ds(start, side), :].astype(jnp.int32),
            first_msg[pl.ds(start, side), :].astype(jnp.int32),
        )
        codes = jnp.where(
            second_half,
            second_msg[2 * side : 2 * side + CODE_ROWS, :].astype(jnp.int32),
            first_msg[2 * side : 2 * side + CODE_ROWS, :].astype(jnp.int32),
        )
        total = total + decoded(q, jnp.where(odd == 1, codes[1:2], codes[0:1]))
    count = counts[b]
    for s in range(4):
        g = total[:, s * side : (s + 1) * side].T
        kept = s < count
        m, v, w = first[b, s], second[b, s], weight[b, s]
        moved_first = beta_one * m + (1.0 - beta_one) * g
        moved_second = beta_two * v + (1.0 - beta_two) * g * g
        step_dir = moved_first / correction_one / (jnp.sqrt(moved_second / correction_two) + adam_eps)
        new_first[0, s] = jnp.where(kept, moved_first, m)
        new_second[0, s] = jnp.where(kept, moved_second, v)
        new_weight[0, s] = jnp.where(kept, w - learn_rate * step_dir, w)


def adam(counts, grads, messages, weight, first, second):
    blocks = weight.shape[0]
    vmem = pl.BlockSpec(memory_space=pltpu.VMEM)
    state = pl.BlockSpec((1,) + weight.shape[1:], lambda b: (b, 0, 0, 0))
    out = jax.ShapeDtypeStruct(weight.shape, jnp.float32)
    return pl.pallas_call(
        adam_kernel,
        out_shape=(out, out, out),
        grid=(blocks,),
        in_specs=[pl.BlockSpec(memory_space=pltpu.SMEM)] + [vmem] * 9,
        out_specs=(state, state, state),
        compiler_params=pltpu.CompilerParams(vmem_limit_bytes=VMEM_LIMIT),
        name="adam",
    )(counts, *grads, *messages, in_vmem(weight), in_vmem(first), in_vmem(second))


def local(features, positives, tile_rows, tile_count, weight, first_moment, second_moment):
    blocks, slots, side = weight.shape[:3]
    depth = slots * side
    rows = features.shape[0]
    z_size = lax.axis_size("blk") // 2
    label_size = lax.axis_size("labels")
    x_size = label_size // 4
    shift = functools.partial(z_shift, z_size=z_size)
    move = functools.partial(moved, z_size=z_size, label_size=label_size)
    blk, label = lax.axis_index("blk"), lax.axis_index("labels")
    x, core = label // 4, label % 2

    with jax.named_scope("rows_of_other_half"):
        part = rows // (4 * x_size)
        at_core = [
            move(lax.dynamic_slice_in_dim(features, ((x * 2 + core) * 2 + k) * part, part, 0), cross=True)
            for k in range(2)
        ]
        places = [(0, 0), (0, 1)]
        left = [move(q, x_by=1) for q in at_core]
        right = [move(q, x_by=-1) for q in at_core]
        far_rows = [move(left[0], x_by=1), move(right[1], x_by=-1)]
        for k in range(2):
            at_core += [left[k], right[k]]
            places += [(-1, k), (1, k)]
        at_core += far_rows
        places += [(2, 0), (2, 1)]
        other = at_core + [move(q, swap=True) for q in at_core]
        order = jnp.stack(
            [(((x + dx) % x_size) * 2 + (core ^ swap)) * 2 + k for swap in range(2) for dx, k in places]
        )
        sorted_pos = jnp.take(positives.reshape(4 * x_size, part, -1), order, axis=0).reshape(rows, -1)
        other_pos = move(sorted_pos.T, cross=True)
        own_pos = positives.T

    with jax.named_scope("kept_tiles"):
        kept = jnp.arange(slots, dtype=jnp.int32)[None, :] < tile_count[:, None]
        tiles = jnp.where(kept[:, :, None, None], weight, 0.0).astype(jnp.bfloat16)
        tiles = tiles.reshape(2, 2 * depth, side)
        ids = jnp.pad(tile_rows.reshape(1, -1), ((0, CODE_ROWS - 1), (0, side - blocks * slots)))
        tiles = jnp.concatenate([tiles[0], ids.astype(jnp.bfloat16), tiles[1]], axis=0)
        cut = 2 * depth + CODE_ROWS

    with jax.named_scope("tiles_round_z"):
        ring = {0: [tiles]}
        up, down = tiles, tiles
        for hop in (1, 2, 3):
            up, down = shift(up, 1), shift(down, -1)
            ring[hop], ring[z_size - hop] = [up], [down]
        ring[4] = [shift(up[:cut], 1), shift(down[cut:], -1)]

    def table_of(j):
        owner = ((blk // 2 - j) % z_size) * 2 + blk % 2
        base = (label * 2 * z_size + owner) * (blocks * side)
        own_ids = ring[j][0][cut - CODE_ROWS, : blocks * slots].astype(jnp.int32)
        return jnp.concatenate([own_ids, base[None]])

    own_slab, other_slab = ([features], own_pos), (other, other_pos)
    with jax.named_scope("own_rows"):
        table = {j: table_of(j) for j in ring}
        early = {j: tile_grads(table[j], [own_slab], ring[j]) for j in (0, 1, 7, 2, 6)}

    with jax.named_scope("sums_round_z"):
        both = [own_slab, other_slab]
        down_a, up_b = tile_grads(table[4], both, ring[4], as_message=(True, True))
        down_a, up_b = shift(down_a, -1), shift(up_b, 1)
        grad_a, down_b = tile_grads(table[3], both, ring[3], as_message=(False, True))
        up_a, grad_b = tile_grads(table[5], both, ring[5], as_message=(True, False))
        down_b, up_a = shift(down_b, -1), shift(up_a, 1)
        down_a, up_b = encode(down_a, grad_a), encode(up_b, grad_b)
        down_a, up_b = shift(down_a, -1), shift(up_b, 1)
        for hop in (2, 1):
            low = tile_grads(table[hop], [other_slab], ring[hop], early[hop])
            high = tile_grads(table[z_size - hop], [other_slab], ring[z_size - hop], early[z_size - hop])
            down_b, up_a = encode(down_b, low[1]), encode(up_a, high[0])
            down_b, up_a = shift(down_b, -1), shift(up_a, 1)
            down_a, up_b = encode(down_a, low[0]), encode(up_b, high[1])
            down_a, up_b = shift(down_a, -1), shift(up_b, 1)
        own = tile_grads(table[0], [other_slab], ring[0], early[0])

    with jax.named_scope("adam"):
        return tuple(
            adam(tile_count, own, [down_a, down_b, up_a, up_b], weight, first_moment, second_moment)
        )


def solution(mesh):
    whole = P(("labels", "blk"), None, None, None)
    return jax.shard_map(
        local,
        mesh=mesh,
        in_specs=(
            P("blk", None),
            P("blk", None),
            P(("labels", "blk"), None),
            P(("labels", "blk")),
            whole,
            whole,
            whole,
        ),
        out_specs=(whole, whole, whole),
        check_vma=False,
    )
```

```python
import functools
import math

import jax
import jax.numpy as jnp
from jax import lax
from jax.experimental import pallas as pl
from jax.experimental.pallas import tpu as pltpu
from jax.sharding import PartitionSpec as P

beta_one = 0.9
beta_two = 0.999
adam_eps = 1e-08
learn_rate = 0.1
correction_one = 1.0 - 0.9**10
correction_two = 1.0 - 0.999**10

STEPS = 8.0
TOP = 32000.0
LN2 = math.log(2.0)
CODE_ROWS = 16
VMEM_LIMIT = 16 * 1024 * 1024


def z_shift(array, by, z_size):
    moves = [(2 * z + h, 2 * ((z + by) % z_size) + h) for z in range(z_size) for h in range(2)]
    return lax.ppermute(array, "blk", moves)


def moved(array, z_size, label_size, cross=False, x_by=0, swap=False):
    moves = []
    for blk in range(2 * z_size):
        for l in range(label_size):
            x, y_lo, core = l // 4, l // 2 % 2, l % 2
            to = ((x + x_by) % (label_size // 4)) * 4 + (y_lo ^ cross) * 2 + (core ^ swap)
            moves.append((blk * label_size + l, (blk ^ cross) * label_size + to))
    return lax.ppermute(array, ("blk", "labels"), moves)


def in_vmem(array):
    return pltpu.with_memory_space_constraint(array, pltpu.VMEM)


def code_of(g):
    top = jnp.maximum(jnp.max(jnp.abs(g), axis=0, keepdims=True), 1e-30)
    return jnp.ceil(jnp.log(top) * (STEPS / LN2))


def coded(g, code):
    q = jnp.round(g * (jnp.exp(code * (-LN2 / STEPS)) * TOP))
    return q.astype(jnp.int32).astype(jnp.int16)


def decoded(q, codes):
    scale = jnp.exp(codes.astype(jnp.float32) * (LN2 / STEPS)) * (1.0 / TOP)
    return q.astype(jnp.int32).astype(jnp.float32) * scale


def store_half(out, grads):
    if out.dtype == jnp.float32:
        for b, g in enumerate(grads):
            out[b] = g
        return
    side, depth = grads[0].shape
    row = lax.broadcasted_iota(jnp.int32, (CODE_ROWS, depth), 0)
    codes = jnp.zeros((CODE_ROWS, depth), jnp.int32)
    for b, g in enumerate(grads):
        code = code_of(g)
        out[side * b : side * (b + 1), :] = coded(g, code)
        codes = jnp.where(row == b, code.astype(jnp.int32), codes)
    out[2 * side : 2 * side + CODE_ROWS, :] = codes.astype(jnp.int16)


def residual(w_t, x, pos, base):
    logits = lax.dot_general(w_t, x, (((1,), (1,)), ((), ())), preferred_element_type=jnp.float32)
    rel = pos - base
    word_of = rel >> 5
    bit = jnp.left_shift(jnp.int32(1), rel & 31)
    sub = lax.broadcasted_iota(jnp.int32, rel.shape, 0)
    hits = []
    for word in range(4):
        m = jnp.where(word_of == word, bit, 0)
        for by in (4, 2, 1):
            m = m | pltpu.roll(m, by, 0)
        for part in range(4):
            hits.append(lax.shift_right_logical(m, sub + 8 * part) & 1)
    targets = jnp.concatenate(hits, axis=0).astype(jnp.float32)
    return (1.0 / (1.0 + jnp.exp(-logits)) - targets).astype(jnp.bfloat16)


def grad_kernel(slabs, n_tiles, with_acc, *refs):
    rows = []
    for pieces in slabs:
        rows.append((refs[:pieces], refs[pieces]))
        refs = refs[pieces + 1 :]
    jobs = []
    for count in n_tiles:
        taken = 1 + count + (2 if with_acc else 0)
        jobs.append((refs[0], refs[1 : 1 + count], refs[1 + count : taken]))
        refs = refs[taken:]
    for (table, tiles, accs), outs in zip(jobs, zip(refs[::2], refs[1::2])):
        side = tiles[0].shape[1]
        depth = 4 * side
        for half in range(2):
            grads = []
            for b in range(2):
                block = 2 * half + b
                columns = [pl.ds(pl.multiple_of(table[block * 4 + s] * side, side), side) for s in range(4)]
                if len(tiles) == 2:
                    w = tiles[half][b * depth : (b + 1) * depth, :]
                else:
                    start = block * depth + (CODE_ROWS if half else 0)
                    w = tiles[0][start : start + depth, :]
                w_t = w.T
                grad = accs[half][b] if with_acc else None
                for pieces, pos in rows:
                    x = jnp.concatenate(
                        [jnp.concatenate([piece[:, c] for c in columns], axis=1) for piece in pieces], axis=0
                    )
                    term = jnp.dot(
                        residual(w_t, x, pos[...], table[16] + block * side), x, preferred_element_type=jnp.float32
                    )
                    grad = term if grad is None else grad + term
                grads.append(grad)
            store_half(outs[half], grads)


def tile_grads(slabs, jobs, accs=None, as_message=((False, False),) * 2):
    vmem = pl.BlockSpec(memory_space=pltpu.VMEM)
    operands, specs = [], []
    for pieces, pos in slabs:
        operands += [in_vmem(piece) for piece in pieces] + [pos]
    specs += [vmem] * len(operands)
    for i, (table, tiles) in enumerate(jobs):
        more = list(tiles) + (list(accs[i]) if accs else [])
        operands += [table] + more
        specs += [pl.BlockSpec(memory_space=pltpu.SMEM)] + [vmem] * len(more)
    side = jobs[0][1][0].shape[1]
    depth = 4 * side
    rows = sum(pos.shape[1] for _, pos in slabs)
    out = pl.pallas_call(
        functools.partial(grad_kernel, [len(p) for p, _ in slabs], [len(t) for _, t in jobs], accs is not None),
        out_shape=[
            jax.ShapeDtypeStruct((2 * side + CODE_ROWS, depth), jnp.int16)
            if message
            else jax.ShapeDtypeStruct((2, side, depth), jnp.float32)
            for messages in as_message[: len(jobs)]
            for message in messages
        ],
        in_specs=specs,
        out_specs=[vmem] * (2 * len(jobs)),
        compiler_params=pltpu.CompilerParams(vmem_limit_bytes=VMEM_LIMIT),
        cost_estimate=pl.CostEstimate(
            flops=48 * len(jobs) * rows * depth * side, bytes_accessed=1 << 20, transcendentals=0
        ),
        name="tile_grads",
    )(*operands)
    return [out[2 * i : 2 * i + 2] for i in range(len(jobs))]


def encode_kernel(*refs):
    for got, grad, out in zip(refs[:2], refs[2:4], refs[4:]):
        side = grad.shape[1]
        got_codes = got[2 * side : 2 * side + CODE_ROWS, :].astype(jnp.int32)
        store_half(
            out, [grad[b] + decoded(got[side * b : side * (b + 1), :], got_codes[b : b + 1]) for b in range(2)]
        )


def encode(got, grads):
    vmem = pl.BlockSpec(memory_space=pltpu.VMEM)
    return pl.pallas_call(
        encode_kernel,
        out_shape=[jax.ShapeDtypeStruct(m.shape, jnp.int16) for m in got],
        in_specs=[vmem] * 4,
        out_specs=[vmem] * 2,
        compiler_params=pltpu.CompilerParams(vmem_limit_bytes=VMEM_LIMIT),
        cost_estimate=pl.CostEstimate(flops=0, bytes_accessed=5 << 20, transcendentals=0),
        name="encode",
    )(*got, *grads)


def adam_kernel(half, counts, grad, low, high, weight, first, second, *rest):
    new_weight, new_first, new_second = rest[-3:]
    b = pl.program_id(0)
    side = grad.shape[1]
    start = pl.multiple_of(b * side, side)
    total = grad[b]
    for msg in (low, high):
        codes = msg[2 * side : 2 * side + CODE_ROWS, :].astype(jnp.int32)
        total = total + decoded(msg[pl.ds(start, side), :], jnp.where(b == 1, codes[1:2], codes[0:1]))
    block = 2 * half + b
    count = counts[block]
    for s in range(4):
        g = total[:, s * side : (s + 1) * side].T
        kept = s < count
        m, v, w = first[block, s], second[block, s], weight[block, s]
        moved_first = beta_one * m + (1.0 - beta_one) * g
        moved_second = beta_two * v + (1.0 - beta_two) * g * g
        step_dir = moved_first * (1.0 / correction_one)
        step_dir = step_dir / (jnp.sqrt(moved_second * (1.0 / correction_two)) + adam_eps)
        new_first[0, s] = jnp.where(kept, moved_first, m)
        new_second[0, s] = jnp.where(kept, moved_second, v)
        new_weight[0, s] = jnp.where(kept, w - learn_rate * step_dir, w)


def adam(half, counts, grad, low, high, weight, first, second, filled=()):
    vmem = pl.BlockSpec(memory_space=pltpu.VMEM)
    state = pl.BlockSpec((1,) + weight.shape[1:], lambda b: (2 * half + b, 0, 0, 0))
    out = jax.ShapeDtypeStruct(weight.shape, jnp.float32)
    return pl.pallas_call(
        functools.partial(adam_kernel, half),
        out_shape=(out, out, out),
        grid=(2,),
        in_specs=[pl.BlockSpec(memory_space=pltpu.SMEM)] + [vmem] * 6 + [pl.BlockSpec(memory_space=pl.ANY)] * len(filled),
        out_specs=(state, state, state),
        input_output_aliases={7 + i: i for i in range(len(filled))},
        compiler_params=pltpu.CompilerParams(vmem_limit_bytes=VMEM_LIMIT),
        cost_estimate=pl.CostEstimate(flops=0, bytes_accessed=4 << 20, transcendentals=0),
        name="adam",
    )(counts, grad, low, high, in_vmem(weight), in_vmem(first), in_vmem(second), *filled)


def local(features, positives, tile_rows, tile_count, weight, first_moment, second_moment):
    blocks, slots, side = weight.shape[:3]
    depth = slots * side
    rows = features.shape[0]
    z_size = lax.axis_size("blk") // 2
    label_size = lax.axis_size("labels")
    x_size = label_size // 4
    shift = functools.partial(z_shift, z_size=z_size)
    move = functools.partial(moved, z_size=z_size, label_size=label_size)
    blk, label = lax.axis_index("blk"), lax.axis_index("labels")
    x, core = label // 4, label % 2

    with jax.named_scope("rows_of_other_half"):
        part = rows // (2 * x_size)
        mine = lax.dynamic_slice_in_dim(features, (x * 2 + core) * part, part, 0)
        mine, weight = lax.optimization_barrier((mine, weight))
        near = move(mine, cross=True)
        order = jnp.stack(
            [
                (((x + dx) % x_size) * 2 + (core ^ swap)) * 2 + k
                for swap in range(2)
                for dx in (0, -1, 1, 2)
                for k in range(2)
            ]
        )
        own_pos = positives.T

    with jax.named_scope("kept_tiles"):
        kept = jnp.arange(slots, dtype=jnp.int32)[None, :] < tile_count[:, None]
        tiles = jnp.where(kept[:, :, None, None], weight, 0.0).astype(jnp.bfloat16)
        tiles = tiles.reshape(2, 2 * depth, side)
        ids = jnp.pad(tile_rows.reshape(1, -1), ((0, CODE_ROWS - 1), (0, side - blocks * slots)))
        tiles = jnp.concatenate([tiles[0], ids.astype(jnp.bfloat16), tiles[1]], axis=0)
        cut = 2 * depth + CODE_ROWS

    def table_of(j, message):
        owner = ((blk // 2 - j) % z_size) * 2 + blk % 2
        base = (label * 2 * z_size + owner) * (blocks * side)
        own_ids = message[cut - CODE_ROWS, : blocks * slots].astype(jnp.int32)
        return jnp.concatenate([own_ids, base[None]])

    with jax.named_scope("tiles_round_z"):
        ring, table = {0: [tiles]}, {0: table_of(0, tiles)}
        up, down = shift(tiles, 1), shift(tiles, -1)
        ring[1], ring[7] = [up], [down]
        up, positives = lax.optimization_barrier((up, positives))
        sorted_pos = jnp.take(positives.reshape(4 * x_size, part // 2, -1), order, axis=0).reshape(rows, -1).T
        other_pos = move(sorted_pos, cross=True)
        near, other_pos = lax.optimization_barrier((near, other_pos))
        own_slab = ([features], own_pos)
        up, down = shift(up, 1), shift(down, -1)
        ring[2], ring[6] = [up], [down]
        table[1], table[7] = table_of(1, ring[1][0]), table_of(7, ring[7][0])
        up, table[1], table[7] = lax.optimization_barrier((up, table[1], table[7]))
        up, down = shift(up, 1), shift(down, -1)
        ring[3], ring[5] = [up], [down]
        ring[4] = [shift(up[:cut], 1), shift(down[cut:], -1)]
        for j in (2, 6, 3, 5, 4):
            table[j] = table_of(j, ring[j][0])

    with jax.named_scope("rows_of_other_half"):
        left, right = move(near, x_by=1), move(near, x_by=-1)
        near_swapped = move(near, swap=True)
        left, near_swapped, table[2], table[6] = lax.optimization_barrier((left, near_swapped, table[2], table[6]))
        far = [move(left[: part // 2], x_by=1), move(right[part // 2 :], x_by=-1)]
        left_next, table[3] = lax.optimization_barrier((left, table[3]))
        left_swapped = move(left_next, swap=True)
        right_next, left_swapped = lax.optimization_barrier((right, left_swapped))
        right_swapped = move(right_next, swap=True)
        far = jnp.concatenate(far, axis=0)
        other = [near, left, right, far, near_swapped, left_swapped, right_swapped, move(far, swap=True)]

    other_slab = (other, other_pos)
    early = {}
    with jax.named_scope("own_rows"):
        for owners in ((1, 7), (2, 6), (3, 5), (4,)):
            for j, sums in zip(owners, tile_grads([own_slab], [(table[j], ring[j]) for j in owners])):
                early[j] = sums

    def both_rows(owners, as_message=((False, False),) * 2):
        jobs = [(table[j], ring[j]) for j in owners]
        return tile_grads([other_slab], jobs, [early[j] for j in owners], as_message)

    def onward(down, up):
        return shift(down, -1), shift(up, 1)

    with jax.named_scope("sums_round_z"):
        (far_sums,) = both_rows((4,), ((True, True),))
        down_a, up_b = onward(*far_sums)
        (grad_a, down_b), (up_a, grad_b) = both_rows((3, 5), ((False, True), (True, False)))
        down_b, up_a = onward(down_b, up_a)
        down_a, up_b = onward(*encode([down_a, up_b], [grad_a, grad_b]))
        for hop in (2, 1):
            low, high = both_rows((hop, z_size - hop))
            down_b, up_a = onward(*encode([down_b, up_a], [low[1], high[0]]))
            down_a, up_b = onward(*encode([down_a, up_b], [low[0], high[1]]))
        (home,) = tile_grads([own_slab, other_slab], [(table[0], ring[0])])

    with jax.named_scope("adam"):
        state = (weight, first_moment, second_moment)
        filled = adam(0, tile_count, home[0], down_a, up_a, *state)
        return tuple(adam(1, tile_count, home[1], down_b, up_b, *state, filled))


def solution(mesh):
    whole = P(("labels", "blk"), None, None, None)
    return jax.shard_map(
        local,
        mesh=mesh,
        in_specs=(
            P("blk", None),
            P("blk", None),
            P(("labels", "blk"), None),
            P(("labels", "blk")),
            whole,
            whole,
            whole,
        ),
        out_specs=(whole, whole, whole),
        check_vma=False,
    )
```

```python
import functools
import math

import jax
import jax.numpy as jnp
from jax import lax
from jax.experimental import pallas as pl
from jax.experimental.pallas import tpu as pltpu
from jax.sharding import PartitionSpec as P

beta_one = 0.9
beta_two = 0.999
adam_eps = 1e-08
learn_rate = 0.1
correction_one = 1.0 - 0.9**10
correction_two = 1.0 - 0.999**10

STEPS = 8.0
TOP = 32000.0
LN2 = math.log(2.0)
CODE_ROWS = 16
VMEM_LIMIT = 16 * 1024 * 1024


def z_shift(array, by, z_size):
    moves = [(2 * z + h, 2 * ((z + by) % z_size) + h) for z in range(z_size) for h in range(2)]
    return lax.ppermute(array, "blk", moves)


def moved(array, z_size, label_size, cross=False, x_by=0, swap=False):
    moves = []
    for blk in range(2 * z_size):
        for l in range(label_size):
            x, y_lo, core = l // 4, l // 2 % 2, l % 2
            to = ((x + x_by) % (label_size // 4)) * 4 + (y_lo ^ cross) * 2 + (core ^ swap)
            moves.append((blk * label_size + l, (blk ^ cross) * label_size + to))
    return lax.ppermute(array, ("blk", "labels"), moves)


def in_vmem(array):
    return pltpu.with_memory_space_constraint(array, pltpu.VMEM)


def code_of(g):
    top = jnp.maximum(jnp.max(jnp.abs(g), axis=0, keepdims=True), 1e-30)
    return jnp.ceil(jnp.log(top) * (STEPS / LN2))


def coded(g, code):
    q = jnp.round(g * (jnp.exp(code * (-LN2 / STEPS)) * TOP))
    return q.astype(jnp.int32).astype(jnp.int16)


def decoded(q, codes):
    scale = jnp.exp(codes.astype(jnp.float32) * (LN2 / STEPS)) * (1.0 / TOP)
    return q.astype(jnp.int32).astype(jnp.float32) * scale


def store_half(out, grads):
    if out.dtype == jnp.float32:
        for b, g in enumerate(grads):
            out[b] = g
        return
    side, depth = grads[0].shape
    row = lax.broadcasted_iota(jnp.int32, (CODE_ROWS, depth), 0)
    codes = jnp.zeros((CODE_ROWS, depth), jnp.int32)
    for b, g in enumerate(grads):
        code = code_of(g)
        out[side * b : side * (b + 1), :] = coded(g, code)
        codes = jnp.where(row == b, code.astype(jnp.int32), codes)
    out[2 * side : 2 * side + CODE_ROWS, :] = codes.astype(jnp.int16)


def residual(w_t, x, pos, base):
    logits = lax.dot_general(w_t, x, (((1,), (1,)), ((), ())), preferred_element_type=jnp.float32)
    rel = pos - base
    word_of = rel >> 5
    bit = jnp.left_shift(jnp.int32(1), rel & 31)
    sub = lax.broadcasted_iota(jnp.int32, rel.shape, 0)
    hits = []
    for word in range(4):
        m = jnp.where(word_of == word, bit, 0)
        for by in (4, 2, 1):
            m = m | pltpu.roll(m, by, 0)
        for part in range(4):
            hits.append(lax.shift_right_logical(m, sub + 8 * part) & 1)
    targets = jnp.concatenate(hits, axis=0).astype(jnp.float32)
    return (1.0 / (1.0 + jnp.exp(-logits)) - targets).astype(jnp.bfloat16)


def grad_kernel(slabs, n_tiles, with_acc, *refs):
    rows = []
    for pieces in slabs:
        rows.append((refs[:pieces], refs[pieces]))
        refs = refs[pieces + 1 :]
    jobs = []
    for count in n_tiles:
        taken = 1 + count + (2 if with_acc else 0)
        jobs.append((refs[0], refs[1 : 1 + count], refs[1 + count : taken]))
        refs = refs[taken:]
    for (table, tiles, accs), outs in zip(jobs, zip(refs[::2], refs[1::2])):
        side = tiles[0].shape[1]
        depth = 4 * side
        for half in range(2):
            grads = []
            for b in range(2):
                block = 2 * half + b
                columns = [pl.ds(pl.multiple_of(table[block * 4 + s] * side, side), side) for s in range(4)]
                if len(tiles) == 2:
                    w = tiles[half][b * depth : (b + 1) * depth, :]
                else:
                    start = block * depth + (CODE_ROWS if half else 0)
                    w = tiles[0][start : start + depth, :]
                w_t = w.T
                grad = accs[half][b] if with_acc else None
                for pieces, pos in rows:
                    x = jnp.concatenate(
                        [jnp.concatenate([piece[:, c] for c in columns], axis=1) for piece in pieces], axis=0
                    )
                    term = jnp.dot(
                        residual(w_t, x, pos[...], table[16] + block * side), x, preferred_element_type=jnp.float32
                    )
                    grad = term if grad is None else grad + term
                grads.append(grad)
            store_half(outs[half], grads)


def tile_grads(slabs, jobs, accs=None, as_message=((False, False),) * 2):
    vmem = pl.BlockSpec(memory_space=pltpu.VMEM)
    operands, specs = [], []
    for pieces, pos in slabs:
        operands += [in_vmem(piece) for piece in pieces] + [pos]
    specs += [vmem] * len(operands)
    for i, (table, tiles) in enumerate(jobs):
        more = list(tiles) + (list(accs[i]) if accs else [])
        operands += [table] + more
        specs += [pl.BlockSpec(memory_space=pltpu.SMEM)] + [vmem] * len(more)
    side = jobs[0][1][0].shape[1]
    depth = 4 * side
    rows = sum(pos.shape[1] for _, pos in slabs)
    out = pl.pallas_call(
        functools.partial(grad_kernel, [len(p) for p, _ in slabs], [len(t) for _, t in jobs], accs is not None),
        out_shape=[
            jax.ShapeDtypeStruct((2 * side + CODE_ROWS, depth), jnp.int16)
            if message
            else jax.ShapeDtypeStruct((2, side, depth), jnp.float32)
            for messages in as_message[: len(jobs)]
            for message in messages
        ],
        in_specs=specs,
        out_specs=[vmem] * (2 * len(jobs)),
        compiler_params=pltpu.CompilerParams(vmem_limit_bytes=VMEM_LIMIT),
        cost_estimate=pl.CostEstimate(
            flops=48 * len(jobs) * rows * depth * side, bytes_accessed=1 << 20, transcendentals=0
        ),
        name="tile_grads",
    )(*operands)
    return [out[2 * i : 2 * i + 2] for i in range(len(jobs))]


def encode_kernel(*refs):
    for got, grad, out in zip(refs[:2], refs[2:4], refs[4:]):
        side = grad.shape[1]
        got_codes = got[2 * side : 2 * side + CODE_ROWS, :].astype(jnp.int32)
        store_half(
            out, [grad[b] + decoded(got[side * b : side * (b + 1), :], got_codes[b : b + 1]) for b in range(2)]
        )


def encode(got, grads):
    vmem = pl.BlockSpec(memory_space=pltpu.VMEM)
    return pl.pallas_call(
        encode_kernel,
        out_shape=[jax.ShapeDtypeStruct(m.shape, jnp.int16) for m in got],
        in_specs=[vmem] * 4,
        out_specs=[vmem] * 2,
        compiler_params=pltpu.CompilerParams(vmem_limit_bytes=VMEM_LIMIT),
        cost_estimate=pl.CostEstimate(flops=0, bytes_accessed=5 << 20, transcendentals=0),
        name="encode",
    )(*got, *grads)


def adam_kernel(half, counts, grad, low, high, weight, first, second, *rest):
    new_weight, new_first, new_second = rest[-3:]
    b = pl.program_id(0)
    side = grad.shape[1]
    start = pl.multiple_of(b * side, side)
    total = grad[b]
    for msg in (low, high):
        codes = msg[2 * side : 2 * side + CODE_ROWS, :].astype(jnp.int32)
        total = total + decoded(msg[pl.ds(start, side), :], jnp.where(b == 1, codes[1:2], codes[0:1]))
    block = 2 * half + b
    count = counts[block]
    for s in range(4):
        g = total[:, s * side : (s + 1) * side].T
        kept = s < count
        m, v, w = first[block, s], second[block, s], weight[block, s]
        moved_first = beta_one * m + (1.0 - beta_one) * g
        moved_second = beta_two * v + (1.0 - beta_two) * g * g
        step_dir = moved_first * (1.0 / correction_one)
        step_dir = step_dir / (jnp.sqrt(moved_second * (1.0 / correction_two)) + adam_eps)
        new_first[0, s] = jnp.where(kept, moved_first, m)
        new_second[0, s] = jnp.where(kept, moved_second, v)
        new_weight[0, s] = jnp.where(kept, w - learn_rate * step_dir, w)


def adam(half, counts, grad, low, high, weight, first, second, filled=()):
    vmem = pl.BlockSpec(memory_space=pltpu.VMEM)
    state = pl.BlockSpec((1,) + weight.shape[1:], lambda b: (2 * half + b, 0, 0, 0))
    out = jax.ShapeDtypeStruct(weight.shape, jnp.float32)
    return pl.pallas_call(
        functools.partial(adam_kernel, half),
        out_shape=(out, out, out),
        grid=(2,),
        in_specs=[pl.BlockSpec(memory_space=pltpu.SMEM)] + [vmem] * 6 + [pl.BlockSpec(memory_space=pl.ANY)] * len(filled),
        out_specs=(state, state, state),
        input_output_aliases={7 + i: i for i in range(len(filled))},
        compiler_params=pltpu.CompilerParams(vmem_limit_bytes=VMEM_LIMIT),
        cost_estimate=pl.CostEstimate(flops=0, bytes_accessed=4 << 20, transcendentals=0),
        name="adam",
    )(counts, grad, low, high, in_vmem(weight), in_vmem(first), in_vmem(second), *filled)


def local(features, positives, tile_rows, tile_count, weight, first_moment, second_moment):
    blocks, slots, side = weight.shape[:3]
    depth = slots * side
    rows = features.shape[0]
    z_size = lax.axis_size("blk") // 2
    label_size = lax.axis_size("labels")
    x_size = label_size // 4
    shift = functools.partial(z_shift, z_size=z_size)
    move = functools.partial(moved, z_size=z_size, label_size=label_size)
    blk, label = lax.axis_index("blk"), lax.axis_index("labels")
    x, core = label // 4, label % 2

    with jax.named_scope("rows_of_other_half"):
        part = rows // (2 * x_size)
        mine = lax.dynamic_slice_in_dim(features, (x * 2 + core) * part, part, 0)
        mine, weight = lax.optimization_barrier((mine, weight))
        near = move(mine, cross=True)
        order = jnp.stack(
            [
                (((x + dx) % x_size) * 2 + (core ^ swap)) * 2 + k
                for swap in range(2)
                for dx in (0, -1, 1, 2)
                for k in range(2)
            ]
        )
        own_pos = positives.T

    with jax.named_scope("kept_tiles"):
        kept = jnp.arange(slots, dtype=jnp.int32)[None, :] < tile_count[:, None]
        tiles = jnp.where(kept[:, :, None, None], weight, 0.0).astype(jnp.bfloat16)
        tiles = tiles.reshape(2, 2 * depth, side)
        ids = jnp.pad(tile_rows.reshape(1, -1), ((0, CODE_ROWS - 1), (0, side - blocks * slots)))
        tiles = jnp.concatenate([tiles[0], ids.astype(jnp.bfloat16), tiles[1]], axis=0)
        cut = 2 * depth + CODE_ROWS

    def table_of(j, message):
        owner = ((blk // 2 - j) % z_size) * 2 + blk % 2
        base = (label * 2 * z_size + owner) * (blocks * side)
        own_ids = message[cut - CODE_ROWS, : blocks * slots].astype(jnp.int32)
        return jnp.concatenate([own_ids, base[None]])

    with jax.named_scope("tiles_round_z"):
        ring, table = {0: [tiles]}, {0: table_of(0, tiles)}
        up, down = shift(tiles, 1), shift(tiles, -1)
        ring[1], ring[7] = [up], [down]
        sorted_pos = jnp.take(positives.reshape(4 * x_size, part // 2, -1), order, axis=0).reshape(rows, -1).T
        up, down, sorted_pos = lax.optimization_barrier((up, down, sorted_pos))
        other_pos = move(sorted_pos, cross=True)
        own_slab = ([features], own_pos)
        up, down = shift(up, 1), shift(down, -1)
        ring[2], ring[6] = [up], [down]
        table[1], table[7] = table_of(1, ring[1][0]), table_of(7, ring[7][0])
        up, table[1], table[7] = lax.optimization_barrier((up, table[1], table[7]))
        up, down = shift(up, 1), shift(down, -1)
        ring[3], ring[5] = [up], [down]
        table[2], table[6] = table_of(2, ring[2][0]), table_of(6, ring[6][0])
        up, down, table[2], table[6] = lax.optimization_barrier((up, down, table[2], table[6]))
        ring[4] = [shift(up[:cut], 1), shift(down[cut:], -1)]
        for j in (3, 5, 4):
            table[j] = table_of(j, ring[j][0])

    with jax.named_scope("rows_of_other_half"):
        left, right = move(near, x_by=1), move(near, x_by=-1)
        near_next, table[1], other_pos = lax.optimization_barrier((near, table[1], other_pos))
        near_swapped = move(near_next, swap=True)
        far = [move(left[: part // 2], x_by=1), move(right[part // 2 :], x_by=-1)]
        left_next, near_swapped, table[3] = lax.optimization_barrier((left, near_swapped, table[3]))
        left_swapped = move(left_next, swap=True)
        right_next, left_swapped = lax.optimization_barrier((right, left_swapped))
        right_swapped = move(right_next, swap=True)
        far = jnp.concatenate(far, axis=0)
        other = [near, left, right, far, near_swapped, left_swapped, right_swapped, move(far, swap=True)]

    other_slab = (other, other_pos)
    early = {}
    with jax.named_scope("own_rows"):
        for owners in ((1, 7), (2, 6)):
            for j, sums in zip(owners, tile_grads([own_slab], [(table[j], ring[j]) for j in owners])):
                early[j] = sums

    def both_rows(owners, as_message=((False, False),) * 2):
        jobs = [(table[j], ring[j]) for j in owners]
        return tile_grads([other_slab], jobs, [early[j] for j in owners], as_message)

    def onward(down, up):
        return shift(down, -1), shift(up, 1)

    with jax.named_scope("sums_round_z"):
        (far_sums,) = tile_grads([own_slab, other_slab], [(table[4], ring[4])], as_message=((True, True),))
        down_a, up_b = onward(*far_sums)
        (grad_a, down_b), (up_a, grad_b) = tile_grads(
            [own_slab, other_slab], [(table[j], ring[j]) for j in (3, 5)], as_message=((False, True), (True, False))
        )
        down_b, up_a = onward(down_b, up_a)
        down_a, up_b = onward(*encode([down_a, up_b], [grad_a, grad_b]))
        for hop in (2, 1):
            low, high = both_rows((hop, z_size - hop))
            down_b, up_a = onward(*encode([down_b, up_a], [low[1], high[0]]))
            down_a, up_b = onward(*encode([down_a, up_b], [low[0], high[1]]))
        (home,) = tile_grads([own_slab, other_slab], [(table[0], ring[0])])

    with jax.named_scope("adam"):
        state = (weight, first_moment, second_moment)
        filled = adam(0, tile_count, home[0], down_a, up_a, *state)
        return tuple(adam(1, tile_count, home[1], down_b, up_b, *state, filled))


def solution(mesh):
    whole = P(("labels", "blk"), None, None, None)
    return jax.shard_map(
        local,
        mesh=mesh,
        in_specs=(
            P("blk", None),
            P("blk", None),
            P(("labels", "blk"), None),
            P(("labels", "blk")),
            whole,
            whole,
            whole,
        ),
        out_specs=(whole, whole, whole),
        check_vma=False,
    )
```
